32 devices in a mesh: region: 8 (over z, y), angle: 4 (over x, core).
Axes of the slice: x: 2, y: 2, z: 4, core: 2. Of those that a mesh axis runs over, the one named last changes fastest.
Arguments:
- volume: float32 [128, 128, 128], P('region'), may hold values from -6 to 6
- blocks: bfloat16 [8192, 128, 128], P(('region', 'angle')), may hold values from -0.1875 to 0.1875
- tile_of: int32 [8192], P(('region', 'angle')), may hold values from 0 to 15
- slot_of: int32 [8192], P(('region', 'angle')), may hold values from 0 to 7
- live_count: int32 [32], P(('region', 'angle')), may hold values from 96 to 256, as said below
- ray_of: int32 [256], P(('region', 'angle')), may hold values from 0 to 7
- sinogram: float32 [256, 128, 128], P(('region', 'angle')), may hold values from -6 to 6
- ray_weight: float32 [256, 128], P(('region', 'angle')), may hold values from 0.5 to 2
- pixel_weight: float32 [128, 128], P('region'), may hold values from 0.1 to 0.5
Outputs:
- updated: float32 [128, 128, 128], P(('region', 'angle'))
- residual: float32 [256, 128, 128], P(('region', 'angle'))
The draws below stay inside these ranges and needn't reach their ends.
Inputs may be any that keep to these rules, and one draw needn't show every extreme that they name: Blocks at positions 256 * d + j with j < live_count[d] are in use, the others are ignored; every device uses at least 96 blocks, and some device uses all 256.
All inputs are finite; a program needn't handle non-finite values.
Results may differ from the reference program's by a relative error of at most 0.0039.
Values may be sent and summed in bfloat16 or wider, within the bound.
No kernel may reach another device: no remote copies, remote signals or barrier semaphores. Data moves between devices by JAX's collectives and lax.ppermute only.
A program may use at most 128 MiB of HBM per device.

```python
import math
import jax
import jax.numpy as jnp
from jax import lax

BLK = 128
SLICES = 128
TILE_DEV = 16
RAY_DEV = 8
CAP = 1
NNZ_DEV = 256
TILES = 128
RAYS = 256
ENTRIES = 8192
SLOTS = 8
MAPS = 256
N_REGION = 8
N_ANGLE = 4
DEVICES = 32


def draw_live_count(key, part):
    key_counts, key_fullest = jax.random.split(jax.random.fold_in(key, 7))
    counts = jax.random.randint(key_counts, (DEVICES,), 3 * NNZ_DEV // 8, NNZ_DEV + 1)
    fullest = jax.random.randint(key_fullest, (), 0, DEVICES)
    return jnp.where(jnp.arange(DEVICES) == fullest, NNZ_DEV, counts).astype(jnp.int32)


def touch_ends(entries, key, smallest, high):
    spot = [jax.random.randint(jax.random.fold_in(key, axis), (), 0, length) for axis, length in enumerate(entries.shape)]
    longest = entries.shape.index(max(entries.shape))
    neighbour = spot[:longest] + [(spot[longest] + 1) % entries.shape[longest]] + spot[longest + 1:]
    return entries.at[tuple(spot)].set(smallest).at[tuple(neighbour)].set(high)


def block_levels(key, extent, cuts, least, largest):
    factor_of, own = 1.0, jax.random.fold_in(key, 6)
    for dim, shards_of in cuts:
        draws = jnp.exp(jax.random.uniform(jax.random.fold_in(own, dim), (shards_of,), jnp.float32, least / len(cuts), largest / len(cuts)))
        factor_of = factor_of * jnp.repeat(draws, extent[dim] // shards_of).reshape([-1 if axis == dim else 1 for axis in range(len(extent))])
    return factor_of


def centred(rng, dims, deviation, limit, shards=(), held_as=jnp.bfloat16):
    drawn = deviation * jax.random.normal(rng, dims, jnp.float32)
    if shards:
        drawn = drawn * block_levels(rng, dims, shards, -0.22, 0.18)
    return jnp.clip(drawn, -limit, limit).astype(held_as)


def setup_inputs(seed: int = 0) -> dict:
    arg_keys = jax.random.split(jax.random.key(seed), 10)
    volume = centred(arg_keys[0], (TILES, SLICES, BLK), 1.0, 6.0, ((0, 8),), jnp.float32)
    blocks = centred(arg_keys[1], (ENTRIES, BLK, BLK), (BLK * 8) ** -0.5, 0.1875, ((0, 32),))
    tile_of = touch_ends(jax.random.randint(arg_keys[2], (ENTRIES,), 0, TILE_DEV), jax.random.fold_in(arg_keys[2], 1), 0, TILE_DEV - 1).astype(jnp.int32)
    slot_of = touch_ends(jax.random.randint(arg_keys[3], (ENTRIES,), 0, SLOTS), jax.random.fold_in(arg_keys[3], 1), 0, SLOTS - 1).astype(jnp.int32)
    live_count = draw_live_count(jax.random.fold_in(arg_keys[9], 71), 0)
    ray_of = touch_ends(jax.random.randint(arg_keys[5], (MAPS,), 0, RAY_DEV), jax.random.fold_in(arg_keys[5], 1), 0, RAY_DEV - 1).astype(jnp.int32)
    sinogram = centred(arg_keys[6], (RAYS, SLICES, BLK), 1.0, 6.0, ((0, 32),), jnp.float32)
    ray_weight = jnp.clip(jnp.exp(math.log(2.0) - 1.3862944 * jax.random.uniform(arg_keys[7], (RAYS, BLK), jnp.float32) ** block_levels(arg_keys[7], (RAYS, BLK), ((0, 32),), -0.2, 0.2)), 0.5, 2.0)
    pixel_weight = jnp.clip(jnp.exp(math.log(0.5) - 1.609438 * jax.random.uniform(arg_keys[8], (TILES, BLK), jnp.float32) ** block_levels(arg_keys[8], (TILES, BLK), ((0, 8),), -0.2, 0.2)), 0.1, 0.5)
    return {"volume": volume, "blocks": blocks, "tile_of": tile_of, "slot_of": slot_of, "live_count": live_count, "ray_of": ray_of, "sinogram": sinogram, "ray_weight": ray_weight, "pixel_weight": pixel_weight}


def reference(volume, blocks, tile_of, slot_of, live_count, ray_of, sinogram, ray_weight, pixel_weight):
    device_ids = jnp.arange(DEVICES, dtype=jnp.int32)
    region_idx = device_ids // N_ANGLE
    angle_idx = device_ids % N_ANGLE
    slot_ids = slot_of.reshape(DEVICES, NNZ_DEV)
    owner_idx = slot_ids // CAP
    target_dev = owner_idx * N_ANGLE + angle_idx[:, None]
    map_index = target_dev * (N_REGION * CAP) + region_idx[:, None] * CAP + slot_ids % CAP
    ray_index = (target_dev * RAY_DEV + ray_of[map_index]).astype(jnp.int32)
    tile_index = (region_idx[:, None] * TILE_DEV + tile_of.reshape(DEVICES, NNZ_DEV)).astype(jnp.int32)
    live_mask = jnp.arange(NNZ_DEV, dtype=jnp.int32)[None, :] < live_count[:, None]
    volume_b = volume.astype(jnp.bfloat16)
    block_sets = blocks.reshape(DEVICES, NNZ_DEV, BLK, BLK)

    def forward(total, inputs):
        block_set, tile_ids, ray_ids, is_live = inputs
        picked = volume_b[tile_ids].astype(jnp.float32)
        product = jnp.einsum("esp,erp->esr", picked, block_set.astype(jnp.float32), precision=lax.Precision.HIGHEST)
        product = jnp.where(is_live[:, None, None], product, jnp.zeros_like(product))
        return total.at[ray_ids].add(product), None

    projection, _ = lax.scan(forward, jnp.zeros((RAYS, SLICES, BLK), jnp.float32), (block_sets, tile_index, ray_index, live_mask))
    residual = ray_weight[:, None, :] * (sinogram - projection)
    residual_b = residual.astype(jnp.bfloat16)

    def backward(total, inputs):
        block_set, tile_ids, ray_ids, is_live = inputs
        slot_rows = residual_b[ray_ids].astype(jnp.float32)
        product = jnp.einsum("esr,erp->esp", slot_rows, block_set.astype(jnp.float32), precision=lax.Precision.HIGHEST)
        product = jnp.where(is_live[:, None, None], product, jnp.zeros_like(product))
        return total.at[tile_ids].add(product), None

    gradient, _ = lax.scan(backward, jnp.zeros((TILES, SLICES, BLK), jnp.float32), (block_sets, tile_index, ray_index, live_mask))
    updated = volume + pixel_weight[:, None, :] * gradient
    return updated, residual
```

```python
import functools

import jax
import jax.numpy as jnp
from jax import lax
from jax.experimental import pallas as pl
from jax.experimental.pallas import tpu as pltpu
from jax.sharding import PartitionSpec as P

CHUNKS = 8
UNROLL = 8
VMEM_LIMIT = 40 * 1024 * 1024
SMEM_SPEC = pl.BlockSpec(memory_space=pltpu.SMEM)
VMEM_SPEC = pl.BlockSpec(memory_space=pltpu.VMEM)
ANY_SPEC = pl.BlockSpec(memory_space=pl.ANY)


def dot_pair(x, y, dims):
    return lax.dot_general(x, y, (dims, ((), ())), preferred_element_type=jnp.float32)


def forward_kernel(per_angle, tile_of, slot_of, live_count, volume, blocks, partial_out, held, back_first, back_second,
                   back_count, volume_b, total, first, second, open_slot, open_tile, sems):
    entries = blocks.shape[0]
    slot_count, tile_rows = partial_out.shape[0], volume.shape[0]
    groups = back_count.shape[0]
    room = back_first.shape[0] // groups
    chunk = entries // CHUNKS
    copies = [
        pltpu.make_async_copy(blocks.at[pl.ds(c * chunk, chunk)], held.at[pl.ds(c * chunk, chunk)], sems.at[c])
        for c in range(CHUNKS)
    ]
    for copy in copies:
        copy.start()
    held[entries] = jnp.zeros(held.shape[1:], held.dtype)
    volume_b[...] = volume[...].astype(jnp.bfloat16)
    total[...] = jnp.zeros_like(total)
    for s in range(slot_count):
        open_slot[s] = -1
    for t in range(tile_rows):
        open_tile[t] = -1
    for g in range(groups):
        back_count[g] = 0
    live = live_count[0]

    def place(e, n):
        s = slot_of[e]
        t = tile_of[e]
        is_live = e < live
        p = open_slot[s]
        first[n] = p
        second[n] = e
        paired = jnp.logical_and(p >= 0, is_live)
        open_slot[s] = jnp.where(is_live, jnp.where(p >= 0, -1, e), p)
        q = open_tile[t]
        g = lax.div(t, per_angle)
        m = back_count[g]
        back_first[g * room + m] = q
        back_second[g * room + m] = e
        back_count[g] = m + jnp.where(jnp.logical_and(q >= 0, is_live), 1, 0)
        open_tile[t] = jnp.where(is_live, jnp.where(q >= 0, -1, e), q)
        return n + jnp.where(paired, 1, 0)

    def multiply(i, _):
        for u in range(UNROLL):
            j = i * UNROLL + u
            a, b = first[j], second[j]
            ka, kb = jnp.minimum(a, entries - 1), jnp.minimum(b, entries - 1)
            s = slot_of[ka]
            left = jnp.concatenate([volume_b[tile_of[ka]], volume_b[tile_of[kb]]], axis=1)
            right = jnp.concatenate([held[a], held[b]], axis=1)
            total[s] += dot_pair(left, right, ((1,), (1,)))
        return 0

    n, done = jnp.int32(0), jnp.int32(0)
    marks = []
    for c in range(CHUNKS):
        n = lax.fori_loop(c * chunk, (c + 1) * chunk, place, n, unroll=8)
        marks.append(n)
    for s in range(slot_count):
        p = open_slot[s]
        first[n] = p
        second[n] = entries
        n = n + jnp.where(p >= 0, 1, 0)
    for u in range(UNROLL):
        first[n + u] = entries
        second[n + u] = entries
    for t in range(tile_rows):
        p = open_tile[t]
        g = t // per_angle
        m = back_count[g]
        back_first[g * room + m] = p
        back_second[g * room + m] = entries
        back_count[g] = m + jnp.where(p >= 0, 1, 0)
    for g in range(groups):
        m = back_count[g]
        for u in range(UNROLL):
            back_first[g * room + m + u] = entries
            back_second[g * room + m + u] = entries
    for c in range(CHUNKS):
        copies[c].wait()
        if c == CHUNKS - 1:
            upto = lax.div(n + (UNROLL - 1), UNROLL)
        else:
            upto = lax.div(marks[c], UNROLL)
        lax.fori_loop(done, upto, multiply, 0)
        done = upto
    partial_out[...] = total[...].astype(partial_out.dtype)


def residual_kernel(ray_of, received, sinogram, ray_weight, residual, outgoing, total):
    total[...] = jnp.zeros_like(total)
    slot_count, ray_rows = received.shape[0], sinogram.shape[0]
    for r in range(slot_count):
        total[ray_of[r]] += received[r].astype(jnp.float32)
    residual[...] = ray_weight[...][:, None, :] * (sinogram[...] - total[...])
    for r in range(slot_count):
        outgoing[r] = residual[ray_of[r]].astype(outgoing.dtype)


def backward_sums(mask, per_angle, me, tile_of, slot_of, back_first, back_second, back_count, held, returned, total):
    entries = tile_of.shape[0]
    groups = back_count.shape[0]
    room = back_first.shape[0] // groups
    g = jnp.bitwise_xor(me[0], mask)
    total[...] = jnp.zeros_like(total)

    def multiply(i, _):
        for u in range(UNROLL):
            j = g * room + i * UNROLL + u
            a, b = back_first[j], back_second[j]
            ka, kb = jnp.minimum(a, entries - 1), jnp.minimum(b, entries - 1)
            t = lax.rem(tile_of[ka], per_angle)
            left = jnp.concatenate([returned[slot_of[ka]], returned[slot_of[kb]]], axis=1)
            right = jnp.concatenate([held[a], held[b]], axis=0)
            total[t] += dot_pair(left, right, ((1,), (0,)))
        return 0

    lax.fori_loop(0, lax.div(back_count[g] + (UNROLL - 1), UNROLL), multiply, 0)


def backward_kernel(mask, per_angle, n_recv, *refs):
    core, recv, (out, total) = refs[:8], refs[8:8 + n_recv], refs[8 + n_recv:]
    backward_sums(mask, per_angle, *core, total)
    value = total[...]
    for piece in recv:
        value = value + piece[...].astype(jnp.float32)
    out[...] = value.astype(out.dtype)


def update_kernel(mask, per_angle, n_recv, *refs):
    core, recv, (volume, weight, out, total) = refs[:8], refs[8:8 + n_recv], refs[8 + n_recv:]
    backward_sums(mask, per_angle, *core, total)
    value = total[...]
    for piece in recv:
        value = value + piece[...].astype(jnp.float32)
    out[...] = volume[...] + weight[...][:, None, :] * value


def body(volume, blocks, tile_of, slot_of, live_count, ray_of, sinogram, ray_weight, pixel_weight):
    n_region = lax.axis_size("region")
    n_angle = lax.axis_size("angle")
    slot_count = ray_of.shape[0]
    capacity = slot_count // n_region
    ray_rows = sinogram.shape[0]
    tile_rows, slices, pixels = volume.shape
    entries, rays, _ = blocks.shape
    per_angle = tile_rows // n_angle
    f32, bf16, i32 = jnp.float32, jnp.bfloat16, jnp.int32
    room = entries // 2 + per_angle + UNROLL
    params = pltpu.CompilerParams(vmem_limit_bytes=VMEM_LIMIT)
    angle = lax.axis_index("angle").astype(i32)

    partial_value, held, back_first, back_second, back_count = pl.pallas_call(
        functools.partial(forward_kernel, per_angle),
        out_shape=(
            jax.ShapeDtypeStruct((slot_count, slices, rays), bf16),
            pltpu.VMEM((entries + 1, rays, pixels), bf16),
            jax.ShapeDtypeStruct((n_angle * room,), i32),
            jax.ShapeDtypeStruct((n_angle * room,), i32),
            jax.ShapeDtypeStruct((n_angle,), i32),
        ),
        in_specs=[SMEM_SPEC, SMEM_SPEC, SMEM_SPEC, VMEM_SPEC, pl.BlockSpec(memory_space=pltpu.HBM)],
        out_specs=(VMEM_SPEC, VMEM_SPEC, SMEM_SPEC, SMEM_SPEC, SMEM_SPEC),
        scratch_shapes=[
            pltpu.VMEM((tile_rows, slices, pixels), bf16),
            pltpu.VMEM((slot_count, slices, rays), f32),
            pltpu.SMEM((entries // 2 + slot_count + UNROLL,), i32),
            pltpu.SMEM((entries // 2 + slot_count + UNROLL,), i32),
            pltpu.SMEM((slot_count,), i32),
            pltpu.SMEM((tile_rows,), i32),
            pltpu.SemaphoreType.DMA((CHUNKS,)),
        ],
        compiler_params=params,
        name="forward",
    )(tile_of, slot_of, live_count, volume, blocks)

    received = lax.all_to_all(
        partial_value.reshape((n_region, capacity, slices, rays)), "region", split_axis=0, concat_axis=0, tiled=True
    ).reshape(slot_count, slices, rays)

    residual, outgoing = pl.pallas_call(
        residual_kernel,
        out_shape=(
            jax.ShapeDtypeStruct((ray_rows, slices, rays), f32),
            jax.ShapeDtypeStruct((slot_count, slices, rays), bf16),
        ),
        in_specs=[SMEM_SPEC, VMEM_SPEC, VMEM_SPEC, VMEM_SPEC],
        out_specs=(VMEM_SPEC, VMEM_SPEC),
        scratch_shapes=[pltpu.VMEM((ray_rows, slices, rays), f32)],
        compiler_params=params,
        name="residual",
    )(ray_of, received, sinogram, ray_weight)

    returned = lax.all_to_all(
        outgoing.reshape((n_region, capacity, slices, rays)), "region", split_axis=0, concat_axis=0, tiled=True
    ).reshape(slot_count, slices, rays)

    core = (angle.reshape(1), tile_of, slot_of, back_first, back_second, back_count, held, returned)
    core_specs = [SMEM_SPEC] * 6 + [VMEM_SPEC] * 2
    first_tile = angle * per_angle
    volume_part = lax.dynamic_slice_in_dim(volume, first_tile, per_angle, 0)
    weight_part = lax.dynamic_slice_in_dim(pixel_weight, first_tile, per_angle, 0)
    scratch = [pltpu.VMEM((per_angle, slices, pixels), f32)]
    inbox = {m: [] for m in range(n_angle)}
    for mask in range(n_angle - 1, 0, -1):
        recv = inbox[mask]
        share = pl.pallas_call(
            functools.partial(backward_kernel, mask, per_angle, len(recv)),
            out_shape=jax.ShapeDtypeStruct((per_angle, slices, pixels), bf16),
            in_specs=core_specs + [VMEM_SPEC] * len(recv),
            out_specs=VMEM_SPEC,
            scratch_shapes=scratch,
            compiler_params=params,
            name=f"backward_{mask}",
        )(*core, *recv)
        hop = mask & -mask
        inbox[mask ^ hop].append(lax.ppermute(share, "angle", [(j, j ^ hop) for j in range(n_angle)]))
    recv = inbox[0]
    updated = pl.pallas_call(
        functools.partial(update_kernel, 0, per_angle, len(recv)),
        out_shape=jax.ShapeDtypeStruct((per_angle, slices, pixels), f32),
        in_specs=core_specs + [VMEM_SPEC] * (len(recv) + 2),
        out_specs=VMEM_SPEC,
        scratch_shapes=scratch,
        compiler_params=params,
        name="update",
    )(*core, *recv, volume_part, weight_part)
    return (updated, residual)


def solution(mesh):
    placed = (
        P("region", None, None),
        P(("region", "angle"), None, None),
        P(("region", "angle")),
        P(("region", "angle")),
        P(("region", "angle")),
        P(("region", "angle")),
        P(("region", "angle"), None, None),
        P(("region", "angle"), None),
        P("region", None),
    )
    return jax.shard_map(
        body,
        mesh=mesh,
        in_specs=placed,
        out_specs=(P(("region", "angle"), None, None), P(("region", "angle"), None, None)),
        check_vma=False,
    )
```

```python
import functools

import jax
import jax.numpy as jnp
from jax import lax
from jax.experimental import pallas as pl
from jax.experimental.pallas import tpu as pltpu
from jax.sharding import PartitionSpec as P

FORWARD_UNROLL = 64
BACKWARD_UNROLL = 16
CHUNKS = 8
SLOT_BIT = 1 << 16
TILE_BIT = 1 << 24
VMEM_LIMIT = 24 * 1024 * 1024
SMEM_SPEC = pl.BlockSpec(memory_space=pltpu.SMEM)
VMEM_SPEC = pl.BlockSpec(memory_space=pltpu.VMEM)
MAYBE_HBM = jax.ShapeDtypeStruct
HBM_SPEC = pl.BlockSpec(memory_space=pltpu.HBM)


def dot(x, y):
    return lax.dot_general(x, y, (((1,), (0,)), ((), ())), preferred_element_type=jnp.float32)


def ceil_div(a, b):
    return lax.div(a + (b - 1), jnp.int32(b))


def split_tile(tile, per_angle):
    if per_angle & (per_angle - 1) == 0:
        return lax.shift_right_logical(tile, per_angle.bit_length() - 1), jnp.bitwise_and(tile, per_angle - 1)
    return lax.div(tile, jnp.int32(per_angle)), lax.rem(tile, jnp.int32(per_angle))


def away(group, me, groups):
    if groups & (groups - 1) == 0:
        return jnp.bitwise_xor(group, me)
    return lax.rem(group - me + groups, jnp.int32(groups))


def forward_kernel(per_angle, groups, room, unroll, live_count, tile_hbm, slot_hbm, volume_hbm, blocks_hbm,
                   partial_out, lists, kept, tile_of, slot_of, volume, volume_b, total, held, sems, block_sems, kept_sem):
    entries = blocks_hbm.shape[0]
    slot_count, tile_rows = partial_out.shape[0], volume.shape[0]
    chunks = block_sems.shape[0]
    chunk = entries // chunks

    def block_copy(c):
        part = pl.ds(c * chunk, chunk)
        return pltpu.make_async_copy(blocks_hbm.at[part], held.at[part], block_sems.at[c])

    small = [
        pltpu.make_async_copy(slot_hbm, slot_of, sems.at[0]),
        pltpu.make_async_copy(tile_hbm, tile_of, sems.at[1]),
        pltpu.make_async_copy(volume_hbm, volume, sems.at[2]),
    ]
    for copy in small:
        copy.start()
    for c in range(chunks):
        block_copy(c).start()
    keep = pltpu.make_async_copy(blocks_hbm, kept, kept_sem)
    keep.start()
    me = lax.axis_index("angle").astype(jnp.int32)
    total[...] = jnp.zeros_like(total)
    for g in range(groups):
        lists[g] = 0
    for copy in small:
        copy.wait()
    live = live_count[0]
    for t in range(tile_rows):
        volume_b[t] = volume[t].T.astype(jnp.bfloat16)

    def step(i, _):
        for u in range(unroll):
            e = i * unroll + u
            if u % chunk == 0:
                block_copy(lax.div(e, jnp.int32(chunk))).wait()
            is_live = e < live
            s, t = slot_of[e], tile_of[e]
            total[jnp.where(is_live, s, slot_count)] += dot(held[e], volume_b[t])
            g, row = split_tile(t, per_angle)
            g = away(g, me, groups)
            m = lists[g]
            lists[groups + g * room + m] = e + s * SLOT_BIT + row * TILE_BIT
            lists[g] = m + is_live.astype(jnp.int32)
        return 0

    steps = ceil_div(live, unroll)
    lax.fori_loop(0, steps, step, 0)
    for g in range(groups):
        m = lists[g]
        for u in range(BACKWARD_UNROLL):
            lists[groups + g * room + m + u] = per_angle * TILE_BIT
    for s in range(slot_count):
        partial_out[s] = total[s].T.astype(partial_out.dtype)
    per_step = unroll // chunk
    lax.fori_loop(steps * per_step, chunks, lambda c, _: (block_copy(c).wait(), 0)[1], 0)
    keep.wait()


def residual_kernel(ray_of, received, sinogram, ray_weight, residual, outgoing, total):
    total[...] = jnp.zeros_like(total)
    slot_count, ray_rows = received.shape[0], sinogram.shape[0]
    for r in range(slot_count):
        total[ray_of[r]] += received[r].astype(jnp.float32)
    residual[...] = ray_weight[...][:, None, :] * (sinogram[...] - total[...])
    for r in range(slot_count):
        outgoing[r] = residual[ray_of[r]].astype(outgoing.dtype)


def backward_sums(mask, groups, per_angle, lists, held, returned, total):
    room = (lists.shape[0] - groups) // groups
    total[...] = jnp.zeros_like(total)
    first = groups + mask * room

    def multiply(i, _):
        for u in range(BACKWARD_UNROLL):
            word = lists[first + i * BACKWARD_UNROLL + u]
            e = jnp.bitwise_and(word, SLOT_BIT - 1)
            s = jnp.bitwise_and(lax.shift_right_logical(word, 16), 255)
            total[lax.shift_right_logical(word, 24)] += dot(returned[s], held[e])
        return 0

    lax.fori_loop(0, ceil_div(lists[mask], BACKWARD_UNROLL), multiply, 0)
    return total[pl.ds(0, per_angle)]


def backward_kernel(mask, groups, n_recv, lists, held, returned, *refs):
    recv, (out, total) = refs[:n_recv], refs[n_recv:]
    value = backward_sums(mask, groups, out.shape[0], lists, held, returned, total)
    for piece in recv:
        value = value + piece[...].astype(jnp.float32)
    out[...] = value.astype(out.dtype)


def own_kernel(groups, lists, held, returned, volume_hbm, weight_hbm, out, weight_out, volume, weight, total, sems):
    per_angle = out.shape[0]
    mine = pl.ds(lax.axis_index("angle").astype(jnp.int32) * per_angle, per_angle)
    copies = [
        pltpu.make_async_copy(volume_hbm.at[mine], volume, sems.at[0]),
        pltpu.make_async_copy(weight_hbm, weight, sems.at[1]),
    ]
    for copy in copies:
        copy.start()
    value = backward_sums(0, groups, per_angle, lists, held, returned, total)
    for copy in copies:
        copy.wait()
    rows = weight[mine][:, None, :]
    weight_out[...] = rows
    out[...] = volume[...] + rows * value


def update_kernel(n_recv, own, weight, *refs):
    recv, out = refs[:n_recv], refs[n_recv]
    value = recv[0][...].astype(jnp.float32)
    for piece in recv[1:]:
        value = value + piece[...].astype(jnp.float32)
    out[...] = own[...] + weight[...] * value


def body(volume, blocks, tile_of, slot_of, live_count, ray_of, sinogram, ray_weight, pixel_weight):
    n_region = lax.axis_size("region")
    n_angle = lax.axis_size("angle")
    slot_count = ray_of.shape[0]
    capacity = slot_count // n_region
    ray_rows = sinogram.shape[0]
    tile_rows, slices, pixels = volume.shape
    entries, rays, _ = blocks.shape
    per_angle = tile_rows // n_angle
    f32, bf16, i32 = jnp.float32, jnp.bfloat16, jnp.int32
    room = entries + BACKWARD_UNROLL
    unroll = min(FORWARD_UNROLL, entries)
    chunks = min(CHUNKS, entries)
    params = pltpu.CompilerParams(vmem_limit_bytes=VMEM_LIMIT)
    in_hbm = functools.partial(pltpu.with_memory_space_constraint, memory_space=pltpu.HBM)
    in_vmem = functools.partial(pltpu.with_memory_space_constraint, memory_space=pltpu.VMEM)
    list_size = n_angle * (room + 1)

    partial_value, lists, kept = pl.pallas_call(
        functools.partial(forward_kernel, per_angle, n_angle, room, unroll),
        out_shape=(
            MAYBE_HBM((slot_count, slices, rays), bf16),
            jax.ShapeDtypeStruct((list_size,), i32),
            pltpu.VMEM(blocks.shape, bf16),
        ),
        in_specs=[SMEM_SPEC] + [HBM_SPEC] * 4,
        out_specs=(VMEM_SPEC, SMEM_SPEC, pl.BlockSpec(memory_space=pl.ANY)),
        scratch_shapes=[
            pltpu.SMEM((entries,), i32),
            pltpu.SMEM((entries,), i32),
            pltpu.VMEM((tile_rows, slices, pixels), f32),
            pltpu.VMEM((tile_rows, slices, pixels), bf16),
            pltpu.VMEM((slot_count + 1, slices, rays), f32),
            pltpu.VMEM((entries, rays, pixels), bf16),
            pltpu.SemaphoreType.DMA((3,)),
            pltpu.SemaphoreType.DMA((chunks,)),
            pltpu.SemaphoreType.DMA,
        ],
        compiler_params=params,
        name="forward",
    )(live_count, *[in_hbm(x) for x in (tile_of, slot_of, volume, blocks)])

    received = lax.all_to_all(
        partial_value.reshape((n_region, capacity, slices, rays)), "region", split_axis=0, concat_axis=0, tiled=True
    ).reshape(slot_count, slices, rays)

    residual, outgoing = pl.pallas_call(
        residual_kernel,
        out_shape=(
            jax.ShapeDtypeStruct((ray_rows, slices, rays), f32),
            MAYBE_HBM((slot_count, slices, rays), bf16),
        ),
        in_specs=[SMEM_SPEC, VMEM_SPEC, VMEM_SPEC, VMEM_SPEC],
        out_specs=(VMEM_SPEC, VMEM_SPEC),
        scratch_shapes=[pltpu.VMEM((ray_rows, slices, rays), f32)],
        compiler_params=params,
        name="residual",
    )(ray_of, received, sinogram, ray_weight)

    returned = lax.all_to_all(
        outgoing.reshape((n_region, capacity, slices, rays)), "region", split_axis=0, concat_axis=0, tiled=True
    ).reshape(slot_count, slices, rays)

    held_in = kept
    held_in = in_vmem(held_in)

    def backward(mask, recv):
        return pl.pallas_call(
            functools.partial(backward_kernel, mask, n_angle, len(recv)),
            out_shape=jax.ShapeDtypeStruct((per_angle, slices, pixels), bf16),
            in_specs=[SMEM_SPEC] + [VMEM_SPEC] * (2 + len(recv)),
            out_specs=VMEM_SPEC,
            scratch_shapes=[pltpu.VMEM((per_angle + 1, slices, pixels), f32)],
            compiler_params=params,
            name=f"backward_{mask}",
        )(lists, held_in, returned, *recv)

    paired = n_angle & (n_angle - 1) == 0
    inbox = {m: [] for m in range(n_angle)}
    for mask in range(n_angle - 1, 0, -1):
        share = backward(mask, inbox[mask])
        if paired:
            hop = mask & -mask
            there = [(j, j ^ hop) for j in range(n_angle)]
            inbox[mask ^ hop].append(lax.ppermute(share, "angle", there))
        else:
            there = [(j, (j + mask) % n_angle) for j in range(n_angle)]
            inbox[0].append(lax.ppermute(share, "angle", there))
    own, weight = pl.pallas_call(
        functools.partial(own_kernel, n_angle),
        out_shape=(
            jax.ShapeDtypeStruct((per_angle, slices, pixels), f32),
            jax.ShapeDtypeStruct((per_angle, 1, pixels), f32),
        ),
        in_specs=[SMEM_SPEC] + [VMEM_SPEC] * 2 + [HBM_SPEC] * 2,
        out_specs=(VMEM_SPEC, VMEM_SPEC),
        scratch_shapes=[
            pltpu.VMEM((per_angle, slices, pixels), f32),
            pltpu.VMEM(pixel_weight.shape, f32),
            pltpu.VMEM((per_angle + 1, slices, pixels), f32),
            pltpu.SemaphoreType.DMA((2,)),
        ],
        compiler_params=params,
        name="own",
    )(lists, held_in, returned, in_hbm(volume), in_hbm(pixel_weight))
    recv = inbox[0]
    updated = pl.pallas_call(
        functools.partial(update_kernel, len(recv)),
        out_shape=jax.ShapeDtypeStruct((per_angle, slices, pixels), f32),
        in_specs=[VMEM_SPEC] * (len(recv) + 2),
        out_specs=VMEM_SPEC,
        compiler_params=params,
        name="update",
    )(own, weight, *recv)
    return (updated, residual)


def solution(mesh):
    placed = (
        P("region", None, None),
        P(("region", "angle"), None, None),
        P(("region", "angle")),
        P(("region", "angle")),
        P(("region", "angle")),
        P(("region", "angle")),
        P(("region", "angle"), None, None),
        P(("region", "angle"), None),
        P("region", None),
    )
    return jax.shard_map(
        body,
        mesh=mesh,
        in_specs=placed,
        out_specs=(P(("region", "angle"), None, None), P(("region", "angle"), None, None)),
        check_vma=False,
    )
```

```python
import functools

import jax
import jax.numpy as jnp
from jax import lax
from jax.experimental import pallas as pl
from jax.experimental.pallas import tpu as pltpu
from jax.sharding import PartitionSpec as P

FORWARD_PARTS = 2
BACKWARD_PAIRS = 16
SLOT_BIT = 1 << 16
TILE_BIT = 1 << 24
VMEM_LIMIT = 24 * 1024 * 1024
SMEM_SPEC = pl.BlockSpec(memory_space=pltpu.SMEM)
VMEM_SPEC = pl.BlockSpec(memory_space=pltpu.VMEM)
MAYBE_HBM = jax.ShapeDtypeStruct
HBM_SPEC = pl.BlockSpec(memory_space=pltpu.HBM)


def dot(x, y):
    return lax.dot_general(x, y, (((1,), (0,)), ((), ())), preferred_element_type=jnp.float32)


def ceil_div(a, b):
    return lax.div(a + (b - 1), jnp.int32(b))


def split_tile(tile, per_angle):
    if per_angle & (per_angle - 1) == 0:
        return lax.shift_right_logical(tile, per_angle.bit_length() - 1), jnp.bitwise_and(tile, per_angle - 1)
    return lax.div(tile, jnp.int32(per_angle)), lax.rem(tile, jnp.int32(per_angle))


def entry_bits(word):
    return jnp.bitwise_and(word, SLOT_BIT - 1)


def slot_bits(word):
    return jnp.bitwise_and(lax.shift_right_logical(word, 16), 255)


def away(group, me, groups):
    if groups & (groups - 1) == 0:
        return jnp.bitwise_xor(group, me)
    return lax.rem(group - me + groups, jnp.int32(groups))


def forward_kernel(per_angle, groups, room, live_count, tile_hbm, slot_hbm, volume_hbm, blocks_hbm,
                   partial_out, lists, kept, tile_of, slot_of, volume, volume_b, total, held, open_tile, sems,
                   block_sems, kept_sem):
    entries = blocks_hbm.shape[0]
    slot_count, tile_rows = partial_out.shape[0], volume.shape[0]
    parts = block_sems.shape[0]
    edges = [entries * c // parts for c in range(parts + 1)]
    small = [
        pltpu.make_async_copy(slot_hbm, slot_of, sems.at[0]),
        pltpu.make_async_copy(tile_hbm, tile_of, sems.at[1]),
        pltpu.make_async_copy(volume_hbm, volume, sems.at[2]),
    ]
    large = []
    for c in range(parts):
        part = pl.ds(edges[c], edges[c + 1] - edges[c])
        large.append(pltpu.make_async_copy(blocks_hbm.at[part], held.at[part], block_sems.at[c]))
    keep = pltpu.make_async_copy(blocks_hbm, kept, kept_sem)
    for copy in small + large + [keep]:
        copy.start()
    me = lax.axis_index("angle").astype(jnp.int32)
    total[...] = jnp.zeros_like(total)
    for g in range(groups):
        lists[g] = 0
    for t in range(tile_rows):
        open_tile[t] = -1
    for copy in small:
        copy.wait()
    live = live_count[0]
    for t in range(tile_rows):
        volume_b[t] = volume[t].T.astype(jnp.bfloat16)

    def list_base(g):
        return groups + g * (2 * room)

    def work(e):
        is_live = e < live
        s, t = slot_of[e], tile_of[e]
        total[jnp.where(is_live, s, slot_count)] += dot(held[e], volume_b[t])
        g, row = split_tile(t, per_angle)
        g = away(g, me, groups)
        word = e + s * SLOT_BIT + row * TILE_BIT
        waiting = open_tile[t]
        paired = waiting >= 0
        m = lists[g]
        at = list_base(g) + 2 * m
        lists[at] = waiting
        lists[at + 1] = word
        lists[g] = m + jnp.logical_and(paired, is_live).astype(jnp.int32)
        open_tile[t] = jnp.where(is_live, jnp.where(paired, -1, word), waiting)

    for c in range(parts):
        large[c].wait()

        @pl.when(edges[c] < live)
        def _(c=c):
            for e in range(edges[c], edges[c + 1]):
                work(e)

    for t in range(tile_rows):
        waiting = open_tile[t]
        g = away(split_tile(jnp.int32(t), per_angle)[0], me, groups)
        m = lists[g]
        at = list_base(g) + 2 * m
        lists[at] = waiting
        lists[at + 1] = slot_count * SLOT_BIT
        lists[g] = m + (waiting >= 0).astype(jnp.int32)
    for g in range(groups):
        at = list_base(g) + 2 * lists[g]
        for u in range(BACKWARD_PAIRS):
            lists[at + 2 * u] = per_angle * TILE_BIT
            lists[at + 2 * u + 1] = 0
    for s in range(slot_count):
        partial_out[s] = total[s].T.astype(partial_out.dtype)
    keep.wait()


def project(ray_of, received, total):
    total[...] = jnp.zeros_like(total)
    for r in range(received.shape[0]):
        total[ray_of[r]] += received[r].astype(jnp.float32)


def outgoing_kernel(ray_of, received, sinogram, ray_weight, outgoing, total, rounded):
    project(ray_of, received, total)
    rounded[...] = (ray_weight[...][:, None, :] * (sinogram[...] - total[...])).astype(rounded.dtype)
    for r in range(received.shape[0]):
        outgoing[r] = rounded[ray_of[r]]


def backward_sums(mask, groups, per_angle, lists, kept, returned, rows, total):
    slot_count = returned.shape[0]
    room = (lists.shape[0] - groups) // (2 * groups)
    rows[pl.ds(0, slot_count)] = returned[...]
    rows[slot_count] = jnp.zeros(rows.shape[1:], rows.dtype)
    total[...] = jnp.zeros_like(total)
    first = groups + mask * (2 * room)

    def multiply(i, _):
        for u in range(BACKWARD_PAIRS):
            at = first + 2 * (i * BACKWARD_PAIRS + u)
            one, two = lists[at], lists[at + 1]
            left = jnp.concatenate([rows[slot_bits(one)], rows[slot_bits(two)]], axis=1)
            right = jnp.concatenate([kept[entry_bits(one)], kept[entry_bits(two)]], axis=0)
            total[lax.shift_right_logical(one, 24)] += dot(left, right)
        return 0

    lax.fori_loop(0, ceil_div(lists[mask], BACKWARD_PAIRS), multiply, 0)
    return total[pl.ds(0, per_angle)]


def backward_kernel(mask, groups, lists, kept, returned, out, rows, total):
    out[...] = backward_sums(mask, groups, out.shape[0], lists, kept, returned, rows, total).astype(out.dtype)


def join_kernel(n_recv, share, *refs):
    recv, out = refs[:n_recv], refs[n_recv]
    value = share[...]
    for piece in recv:
        value = value + piece[...].astype(jnp.float32)
    out[...] = value.astype(out.dtype)


def own_kernel(groups, lists, ray_of, kept, returned, received, sinogram, ray_weight, volume_hbm, weight_hbm,
               out, weight_out, residual, rows, volume, weight, total, rays, sems):
    per_angle = out.shape[0]
    mine = pl.ds(lax.axis_index("angle").astype(jnp.int32) * per_angle, per_angle)
    copies = [
        pltpu.make_async_copy(volume_hbm.at[mine], volume, sems.at[0]),
        pltpu.make_async_copy(weight_hbm, weight, sems.at[1]),
    ]
    for copy in copies:
        copy.start()
    project(ray_of, received, rays)
    rays[...] = ray_weight[...][:, None, :] * (sinogram[...] - rays[...])
    away_copy = pltpu.make_async_copy(rays, residual, sems.at[2])
    away_copy.start()
    value = backward_sums(0, groups, per_angle, lists, kept, returned, rows, total)
    for copy in copies:
        copy.wait()
    scale = weight[mine][:, None, :]
    weight_out[...] = scale
    out[...] = volume[...] + scale * value
    away_copy.wait()


def update_kernel(n_recv, own, weight, *refs):
    recv, out = refs[:n_recv], refs[n_recv]
    value = recv[0][...].astype(jnp.float32)
    for piece in recv[1:]:
        value = value + piece[...].astype(jnp.float32)
    out[...] = own[...] + weight[...] * value


def body(volume, blocks, tile_of, slot_of, live_count, ray_of, sinogram, ray_weight, pixel_weight):
    n_region = lax.axis_size("region")
    n_angle = lax.axis_size("angle")
    slot_count = ray_of.shape[0]
    capacity = slot_count // n_region
    ray_rows = sinogram.shape[0]
    tile_rows, slices, pixels = volume.shape
    entries, rays, _ = blocks.shape
    per_angle = tile_rows // n_angle
    f32, bf16, i32 = jnp.float32, jnp.bfloat16, jnp.int32
    room = entries // 2 + per_angle + BACKWARD_PAIRS
    parts = min(FORWARD_PARTS, entries)
    params = pltpu.CompilerParams(vmem_limit_bytes=VMEM_LIMIT)
    in_hbm = functools.partial(pltpu.with_memory_space_constraint, memory_space=pltpu.HBM)
    in_vmem = functools.partial(pltpu.with_memory_space_constraint, memory_space=pltpu.VMEM)
    list_size = n_angle * (2 * room + 1)

    partial_value, lists, kept = pl.pallas_call(
        functools.partial(forward_kernel, per_angle, n_angle, room),
        out_shape=(
            MAYBE_HBM((slot_count, slices, rays), bf16),
            jax.ShapeDtypeStruct((list_size,), i32),
            pltpu.VMEM(blocks.shape, bf16),
        ),
        in_specs=[SMEM_SPEC] + [HBM_SPEC] * 4,
        out_specs=(VMEM_SPEC, SMEM_SPEC, pl.BlockSpec(memory_space=pl.ANY)),
        scratch_shapes=[
            pltpu.SMEM((entries,), i32),
            pltpu.SMEM((entries,), i32),
            pltpu.VMEM((tile_rows, slices, pixels), f32),
            pltpu.VMEM((tile_rows, slices, pixels), bf16),
            pltpu.VMEM((slot_count + 1, slices, rays), f32),
            pltpu.VMEM((entries, rays, pixels), bf16),
            pltpu.SMEM((tile_rows,), i32),
            pltpu.SemaphoreType.DMA((3,)),
            pltpu.SemaphoreType.DMA((parts,)),
            pltpu.SemaphoreType.DMA,
        ],
        compiler_params=params,
        name="forward",
    )(live_count, *[in_hbm(x) for x in (tile_of, slot_of, volume, blocks)])

    received = lax.all_to_all(
        partial_value.reshape((n_region, capacity, slices, rays)), "region", split_axis=0, concat_axis=0, tiled=True
    ).reshape(slot_count, slices, rays)

    outgoing = pl.pallas_call(
        outgoing_kernel,
        out_shape=jax.ShapeDtypeStruct((slot_count, slices, rays), bf16),
        in_specs=[SMEM_SPEC, VMEM_SPEC, VMEM_SPEC, VMEM_SPEC],
        out_specs=VMEM_SPEC,
        scratch_shapes=[
            pltpu.VMEM((ray_rows, slices, rays), f32),
            pltpu.VMEM((ray_rows, slices, rays), bf16),
        ],
        compiler_params=params,
        name="outgoing",
    )(ray_of, received, sinogram, ray_weight)

    returned = lax.all_to_all(
        outgoing.reshape((n_region, capacity, slices, rays)), "region", split_axis=0, concat_axis=0, tiled=True
    ).reshape(slot_count, slices, rays)

    kept = in_vmem(kept)
    tile_shape = (per_angle, slices, pixels)
    work = [pltpu.VMEM((slot_count + 1, slices, rays), bf16), pltpu.VMEM((per_angle + 1, slices, pixels), f32)]

    def backward(mask, rows, out_type):
        return pl.pallas_call(
            functools.partial(backward_kernel, mask, n_angle),
            out_shape=jax.ShapeDtypeStruct(tile_shape, out_type),
            in_specs=[SMEM_SPEC] + [VMEM_SPEC] * 2,
            out_specs=VMEM_SPEC,
            scratch_shapes=work,
            compiler_params=params,
            name=f"backward_{mask}",
        )(lists, kept, rows)

    paired = n_angle & (n_angle - 1) == 0
    inbox = {m: [] for m in range(n_angle)}
    rows = returned
    for mask in range(n_angle - 1, 0, -1):
        recv = inbox[mask]
        share = backward(mask, rows, f32 if recv else bf16)
        if recv:
            share = pl.pallas_call(
                functools.partial(join_kernel, len(recv)),
                out_shape=jax.ShapeDtypeStruct(tile_shape, bf16),
                in_specs=[VMEM_SPEC] * (1 + len(recv)),
                out_specs=VMEM_SPEC,
                compiler_params=params,
                name=f"join_{mask}",
            )(share, *recv)
            share, rows = lax.optimization_barrier((share, rows))
        hop = mask & -mask if paired else mask
        there = [(j, j ^ hop if paired else (j + hop) % n_angle) for j in range(n_angle)]
        inbox[mask ^ hop if paired else 0].append(lax.ppermute(share, "angle", there))
    own, weight, residual = pl.pallas_call(
        functools.partial(own_kernel, n_angle),
        out_shape=(
            jax.ShapeDtypeStruct(tile_shape, f32),
            jax.ShapeDtypeStruct((per_angle, 1, pixels), f32),
            jax.ShapeDtypeStruct((ray_rows, slices, rays), f32),
        ),
        in_specs=[SMEM_SPEC] * 2 + [VMEM_SPEC] * 5 + [HBM_SPEC] * 2,
        out_specs=(VMEM_SPEC, VMEM_SPEC, HBM_SPEC),
        scratch_shapes=[
            work[0],
            pltpu.VMEM(tile_shape, f32),
            pltpu.VMEM(pixel_weight.shape, f32),
            work[1],
            pltpu.VMEM((ray_rows, slices, rays), f32),
            pltpu.SemaphoreType.DMA((3,)),
        ],
        compiler_params=params,
        name="own",
    )(lists, ray_of, kept, rows, received, sinogram, ray_weight, in_hbm(volume), in_hbm(pixel_weight))
    recv = inbox[0]
    updated = pl.pallas_call(
        functools.partial(update_kernel, len(recv)),
        out_shape=jax.ShapeDtypeStruct((per_angle, slices, pixels), f32),
        in_specs=[VMEM_SPEC] * (len(recv) + 2),
        out_specs=VMEM_SPEC,
        compiler_params=params,
        name="update",
    )(own, weight, *recv)
    return (updated, residual)


def solution(mesh):
    placed = (
        P("region", None, None),
        P(("region", "angle"), None, None),
        P(("region", "angle")),
        P(("region", "angle")),
        P(("region", "angle")),
        P(("region", "angle")),
        P(("region", "angle"), None, None),
        P(("region", "angle"), None),
        P("region", None),
    )
    return jax.shard_map(
        body,
        mesh=mesh,
        in_specs=placed,
        out_specs=(P(("region", "angle"), None, None), P(("region", "angle"), None, None)),
        check_vma=False,
    )
```

```python
import functools

import jax
import jax.numpy as jnp
from jax import lax
from jax.experimental import pallas as pl
from jax.experimental.pallas import tpu as pltpu
from jax.sharding import PartitionSpec as P

FORWARD_PARTS = 2
BACKWARD_PAIRS = 16
SLOT_BIT = 1 << 16
TILE_BIT = 1 << 24
VMEM_LIMIT = 24 * 1024 * 1024
SMEM_SPEC = pl.BlockSpec(memory_space=pltpu.SMEM)
VMEM_SPEC = pl.BlockSpec(memory_space=pltpu.VMEM)
MAYBE_HBM = jax.ShapeDtypeStruct
HBM_SPEC = pl.BlockSpec(memory_space=pltpu.HBM)


def dot(x, y):
    return lax.dot_general(x, y, (((1,), (0,)), ((), ())), preferred_element_type=jnp.float32)


def ceil_div(a, b):
    return lax.div(a + (b - 1), jnp.int32(b))


def split_tile(tile, per_angle):
    if per_angle & (per_angle - 1) == 0:
        return lax.shift_right_logical(tile, per_angle.bit_length() - 1), jnp.bitwise_and(tile, per_angle - 1)
    return lax.div(tile, jnp.int32(per_angle)), lax.rem(tile, jnp.int32(per_angle))


def entry_bits(word):
    return jnp.bitwise_and(word, SLOT_BIT - 1)


def slot_bits(word):
    return jnp.bitwise_and(lax.shift_right_logical(word, 16), 255)


def away(group, me, groups):
    if groups & (groups - 1) == 0:
        return jnp.bitwise_xor(group, me)
    return lax.rem(group - me + groups, jnp.int32(groups))


def forward_kernel(per_angle, groups, room, live_count, tile_hbm, slot_hbm, ray_hbm, volume_hbm, blocks_hbm,
                   partial_out, lists, rays, kept, tile_of, slot_of, volume, volume_b, total, held, open_tile, sems,
                   block_sems, kept_sem):
    entries = blocks_hbm.shape[0]
    slot_count, tile_rows = partial_out.shape[0], volume.shape[0]
    parts = block_sems.shape[0]
    edges = [entries * c // parts for c in range(parts + 1)]
    small = [
        pltpu.make_async_copy(slot_hbm, slot_of, sems.at[0]),
        pltpu.make_async_copy(tile_hbm, tile_of, sems.at[1]),
        pltpu.make_async_copy(volume_hbm, volume, sems.at[2]),
        pltpu.make_async_copy(ray_hbm, rays, sems.at[3]),
    ]
    large = []
    for c in range(parts):
        part = pl.ds(edges[c], edges[c + 1] - edges[c])
        large.append(pltpu.make_async_copy(blocks_hbm.at[part], held.at[part], block_sems.at[c]))
    keep = pltpu.make_async_copy(blocks_hbm, kept, kept_sem)
    for copy in small + large + [keep]:
        copy.start()
    me = lax.axis_index("angle").astype(jnp.int32)
    total[...] = jnp.zeros_like(total)
    for g in range(groups):
        lists[g] = 0
    for t in range(tile_rows):
        open_tile[t] = -1
    for copy in small:
        copy.wait()
    live = live_count[0]
    for t in range(tile_rows):
        volume_b[t] = volume[t].T.astype(jnp.bfloat16)

    def list_base(g):
        return groups + g * (2 * room)

    def work(e):
        is_live = e < live
        s, t = slot_of[e], tile_of[e]
        total[jnp.where(is_live, s, slot_count)] += dot(held[e], volume_b[t])
        g, row = split_tile(t, per_angle)
        g = away(g, me, groups)
        word = e + s * SLOT_BIT + row * TILE_BIT
        waiting = open_tile[t]
        paired = waiting >= 0
        m = lists[g]
        at = list_base(g) + 2 * m
        lists[at] = waiting
        lists[at + 1] = word
        lists[g] = m + jnp.logical_and(paired, is_live).astype(jnp.int32)
        open_tile[t] = jnp.where(is_live, jnp.where(paired, -1, word), waiting)

    for c in range(parts):
        large[c].wait()

        @pl.when(edges[c] < live)
        def _(c=c):
            for e in range(edges[c], edges[c + 1]):
                work(e)

    for t in range(tile_rows):
        waiting = open_tile[t]
        g = away(split_tile(jnp.int32(t), per_angle)[0], me, groups)
        m = lists[g]
        at = list_base(g) + 2 * m
        lists[at] = waiting
        lists[at + 1] = slot_count * SLOT_BIT
        lists[g] = m + (waiting >= 0).astype(jnp.int32)
    for g in range(groups):
        at = list_base(g) + 2 * lists[g]
        for u in range(BACKWARD_PAIRS):
            lists[at + 2 * u] = per_angle * TILE_BIT
            lists[at + 2 * u + 1] = 0
    for s in range(slot_count):
        partial_out[s] = total[s].T.astype(partial_out.dtype)
    keep.wait()


def project(ray_of, received, total):
    total[...] = jnp.zeros_like(total)
    for r in range(received.shape[0]):
        total[ray_of[r]] += received[r].astype(jnp.float32)


def outgoing_kernel(ray_of, received, sinogram, ray_weight, outgoing, total, rounded):
    project(ray_of, received, total)
    rounded[...] = (ray_weight[...][:, None, :] * (sinogram[...] - total[...])).astype(rounded.dtype)
    for r in range(received.shape[0]):
        outgoing[r] = rounded[ray_of[r]]


def backward_sums(mask, groups, per_angle, lists, kept, returned, rows, total):
    slot_count = returned.shape[0]
    room = (lists.shape[0] - groups) // (2 * groups)
    rows[pl.ds(0, slot_count)] = returned[...]
    rows[slot_count] = jnp.zeros(rows.shape[1:], rows.dtype)
    total[...] = jnp.zeros_like(total)
    first = groups + mask * (2 * room)

    def multiply(i, _):
        for u in range(BACKWARD_PAIRS):
            at = first + 2 * (i * BACKWARD_PAIRS + u)
            one, two = lists[at], lists[at + 1]
            left = jnp.concatenate([rows[slot_bits(one)], rows[slot_bits(two)]], axis=1)
            right = jnp.concatenate([kept[entry_bits(one)], kept[entry_bits(two)]], axis=0)
            total[lax.shift_right_logical(one, 24)] += dot(left, right)
        return 0

    lax.fori_loop(0, ceil_div(lists[mask], BACKWARD_PAIRS), multiply, 0)
    return total[pl.ds(0, per_angle)]


def backward_kernel(mask, groups, lists, kept, returned, out, rows, total):
    out[...] = backward_sums(mask, groups, out.shape[0], lists, kept, returned, rows, total).astype(out.dtype)


def join_kernel(n_recv, share, *refs):
    recv, out = refs[:n_recv], refs[n_recv]
    value = share[...]
    for piece in recv:
        value = value + piece[...].astype(jnp.float32)
    out[...] = value.astype(out.dtype)


def own_kernel(groups, lists, ray_of, kept, returned, received, sinogram, ray_weight, volume_hbm, weight_hbm,
               out, weight_out, residual, rows, volume, weight, total, rays, sems):
    per_angle = out.shape[0]
    mine = pl.ds(lax.axis_index("angle").astype(jnp.int32) * per_angle, per_angle)
    copies = [
        pltpu.make_async_copy(volume_hbm.at[mine], volume, sems.at[0]),
        pltpu.make_async_copy(weight_hbm, weight, sems.at[1]),
    ]
    for copy in copies:
        copy.start()
    project(ray_of, received, rays)
    rays[...] = ray_weight[...][:, None, :] * (sinogram[...] - rays[...])
    away_copy = pltpu.make_async_copy(rays, residual, sems.at[2])
    away_copy.start()
    value = backward_sums(0, groups, per_angle, lists, kept, returned, rows, total)
    for copy in copies:
        copy.wait()
    scale = weight[mine][:, None, :]
    weight_out[...] = scale
    out[...] = volume[...] + scale * value
    away_copy.wait()


def update_kernel(n_recv, own, weight, *refs):
    recv, out = refs[:n_recv], refs[n_recv]
    value = recv[0][...].astype(jnp.float32)
    for piece in recv[1:]:
        value = value + piece[...].astype(jnp.float32)
    out[...] = own[...] + weight[...] * value


def body(volume, blocks, tile_of, slot_of, live_count, ray_of, sinogram, ray_weight, pixel_weight):
    n_region = lax.axis_size("region")
    n_angle = lax.axis_size("angle")
    slot_count = ray_of.shape[0]
    capacity = slot_count // n_region
    ray_rows = sinogram.shape[0]
    tile_rows, slices, pixels = volume.shape
    entries, rays, _ = blocks.shape
    per_angle = tile_rows // n_angle
    f32, bf16, i32 = jnp.float32, jnp.bfloat16, jnp.int32
    room = entries // 2 + per_angle + BACKWARD_PAIRS
    parts = min(FORWARD_PARTS, entries)
    params = pltpu.CompilerParams(vmem_limit_bytes=VMEM_LIMIT)
    in_hbm = functools.partial(pltpu.with_memory_space_constraint, memory_space=pltpu.HBM)
    in_vmem = functools.partial(pltpu.with_memory_space_constraint, memory_space=pltpu.VMEM)
    list_size = n_angle * (2 * room + 1)

    partial_value, lists, rays_of, kept = pl.pallas_call(
        functools.partial(forward_kernel, per_angle, n_angle, room),
        out_shape=(
            MAYBE_HBM((slot_count, slices, rays), bf16),
            pltpu.SMEM((list_size,), i32),
            pltpu.SMEM((slot_count,), i32),
            pltpu.VMEM(blocks.shape, bf16),
        ),
        in_specs=[SMEM_SPEC] + [HBM_SPEC] * 5,
        out_specs=(VMEM_SPEC, SMEM_SPEC, SMEM_SPEC, pl.BlockSpec(memory_space=pl.ANY)),
        scratch_shapes=[
            pltpu.SMEM((entries,), i32),
            pltpu.SMEM((entries,), i32),
            pltpu.VMEM((tile_rows, slices, pixels), f32),
            pltpu.VMEM((tile_rows, slices, pixels), bf16),
            pltpu.VMEM((slot_count + 1, slices, rays), f32),
            pltpu.VMEM((entries, rays, pixels), bf16),
            pltpu.SMEM((tile_rows,), i32),
            pltpu.SemaphoreType.DMA((4,)),
            pltpu.SemaphoreType.DMA((parts,)),
            pltpu.SemaphoreType.DMA,
        ],
        compiler_params=params,
        name="forward",
    )(live_count, *[in_hbm(x) for x in (tile_of, slot_of, ray_of, volume, blocks)])

    received = lax.all_to_all(
        partial_value.reshape((n_region, capacity, slices, rays)), "region", split_axis=0, concat_axis=0, tiled=True
    ).reshape(slot_count, slices, rays)

    outgoing = pl.pallas_call(
        outgoing_kernel,
        out_shape=jax.ShapeDtypeStruct((slot_count, slices, rays), bf16),
        in_specs=[SMEM_SPEC, VMEM_SPEC, VMEM_SPEC, VMEM_SPEC],
        out_specs=VMEM_SPEC,
        scratch_shapes=[
            pltpu.VMEM((ray_rows, slices, rays), f32),
            pltpu.VMEM((ray_rows, slices, rays), bf16),
        ],
        compiler_params=params,
        name="outgoing",
    )(rays_of, received, sinogram, ray_weight)

    returned = lax.all_to_all(
        outgoing.reshape((n_region, capacity, slices, rays)), "region", split_axis=0, concat_axis=0, tiled=True
    ).reshape(slot_count, slices, rays)

    kept = in_vmem(kept)
    tile_shape = (per_angle, slices, pixels)
    work = [pltpu.VMEM((slot_count + 1, slices, rays), bf16), pltpu.VMEM((per_angle + 1, slices, pixels), f32)]

    def backward(mask, rows, out_type):
        return pl.pallas_call(
            functools.partial(backward_kernel, mask, n_angle),
            out_shape=jax.ShapeDtypeStruct(tile_shape, out_type),
            in_specs=[SMEM_SPEC] + [VMEM_SPEC] * 2,
            out_specs=VMEM_SPEC,
            scratch_shapes=work,
            compiler_params=params,
            name=f"backward_{mask}",
        )(lists, kept, rows)

    paired = n_angle & (n_angle - 1) == 0
    inbox = {m: [] for m in range(n_angle)}
    rows = returned
    for mask in range(n_angle - 1, 0, -1):
        recv = inbox[mask]
        share = backward(mask, rows, f32 if recv else bf16)
        if recv:
            share = pl.pallas_call(
                functools.partial(join_kernel, len(recv)),
                out_shape=jax.ShapeDtypeStruct(tile_shape, bf16),
                in_specs=[VMEM_SPEC] * (1 + len(recv)),
                out_specs=VMEM_SPEC,
                compiler_params=params,
                name=f"join_{mask}",
            )(share, *recv)
            share, rows = lax.optimization_barrier((share, rows))
        hop = mask & -mask if paired else mask
        there = [(j, j ^ hop if paired else (j + hop) % n_angle) for j in range(n_angle)]
        inbox[mask ^ hop if paired else 0].append(lax.ppermute(share, "angle", there))
    own, weight, residual = pl.pallas_call(
        functools.partial(own_kernel, n_angle),
        out_shape=(
            jax.ShapeDtypeStruct(tile_shape, f32),
            jax.ShapeDtypeStruct((per_angle, 1, pixels), f32),
            jax.ShapeDtypeStruct((ray_rows, slices, rays), f32),
        ),
        in_specs=[SMEM_SPEC] * 2 + [VMEM_SPEC] * 5 + [HBM_SPEC] * 2,
        out_specs=(VMEM_SPEC, VMEM_SPEC, HBM_SPEC),
        scratch_shapes=[
            work[0],
            pltpu.VMEM(tile_shape, f32),
            pltpu.VMEM(pixel_weight.shape, f32),
            work[1],
            pltpu.VMEM((ray_rows, slices, rays), f32),
            pltpu.SemaphoreType.DMA((3,)),
        ],
        compiler_params=params,
        name="own",
    )(lists, rays_of, kept, rows, received, sinogram, ray_weight, in_hbm(volume), in_hbm(pixel_weight))
    recv = inbox[0]
    updated = pl.pallas_call(
        functools.partial(update_kernel, len(recv)),
        out_shape=jax.ShapeDtypeStruct((per_angle, slices, pixels), f32),
        in_specs=[VMEM_SPEC] * (len(recv) + 2),
        out_specs=VMEM_SPEC,
        compiler_params=params,
        name="update",
    )(own, weight, *recv)
    return (updated, residual)


def solution(mesh):
    placed = (
        P("region", None, None),
        P(("region", "angle"), None, None),
        P(("region", "angle")),
        P(("region", "angle")),
        P(("region", "angle")),
        P(("region", "angle")),
        P(("region", "angle"), None, None),
        P(("region", "angle"), None),
        P("region", None),
    )
    return jax.shard_map(
        body,
        mesh=mesh,
        in_specs=placed,
        out_specs=(P(("region", "angle"), None, None), P(("region", "angle"), None, None)),
        check_vma=False,
    )
```

```python
import functools

import jax
import jax.numpy as jnp
from jax import lax
from jax.experimental import pallas as pl
from jax.experimental.pallas import tpu as pltpu
from jax.sharding import PartitionSpec as P

FORWARD_PARTS = 3
BACKWARD_PAIRS = 16
SLOT_BIT = 1 << 16
TILE_BIT = 1 << 24
VMEM_LIMIT = 24 * 1024 * 1024
SMEM_SPEC = pl.BlockSpec(memory_space=pltpu.SMEM)
VMEM_SPEC = pl.BlockSpec(memory_space=pltpu.VMEM)
MAYBE_HBM = jax.ShapeDtypeStruct
HBM_SPEC = pl.BlockSpec(memory_space=pltpu.HBM)


def dot(x, y):
    return lax.dot_general(x, y, (((1,), (0,)), ((), ())), preferred_element_type=jnp.float32)


def ceil_div(a, b):
    return lax.div(a + (b - 1), jnp.int32(b))


def split_tile(tile, per_angle):
    if per_angle & (per_angle - 1) == 0:
        return lax.shift_right_logical(tile, per_angle.bit_length() - 1), jnp.bitwise_and(tile, per_angle - 1)
    return lax.div(tile, jnp.int32(per_angle)), lax.rem(tile, jnp.int32(per_angle))


def entry_bits(word):
    return jnp.bitwise_and(word, SLOT_BIT - 1)


def slot_bits(word):
    return jnp.bitwise_and(lax.shift_right_logical(word, 16), 255)


def away(group, me, groups):
    if groups & (groups - 1) == 0:
        return jnp.bitwise_xor(group, me)
    return lax.rem(group - me + groups, jnp.int32(groups))


def forward_kernel(per_angle, groups, room, live_count, tile_hbm, slot_hbm, ray_hbm, volume_hbm, blocks_hbm, held,
                   partial_out, lists, rays, kept, tile_of, slot_of, volume, volume_b, total, open_tile, sems, block_sems):
    entries = blocks_hbm.shape[0]
    slot_count, tile_rows = partial_out.shape[0], volume.shape[0]
    parts = block_sems.shape[0]
    edges = [entries * c // parts for c in range(parts + 1)]
    small = [
        pltpu.make_async_copy(slot_hbm, slot_of, sems.at[0]),
        pltpu.make_async_copy(tile_hbm, tile_of, sems.at[1]),
        pltpu.make_async_copy(volume_hbm, volume, sems.at[2]),
        pltpu.make_async_copy(ray_hbm, rays, sems.at[3]),
    ]
    large = []
    for c in range(parts):
        part = pl.ds(edges[c], edges[c + 1] - edges[c])
        large.append(pltpu.make_async_copy(blocks_hbm.at[part], kept.at[part], block_sems.at[c]))
    for copy in small + large:
        copy.start()
    me = lax.axis_index("angle").astype(jnp.int32)
    total[...] = jnp.zeros_like(total)
    for g in range(groups):
        lists[g] = 0
    for t in range(tile_rows):
        open_tile[t] = -1
    for copy in small:
        copy.wait()
    live = live_count[0]
    for t in range(tile_rows):
        volume_b[t] = volume[t].T.astype(jnp.bfloat16)

    def list_base(g):
        return groups + g * (2 * room)

    def work(e):
        is_live = e < live
        s, t = slot_of[e], tile_of[e]
        total[jnp.where(is_live, s, slot_count)] += dot(held[e], volume_b[t])
        g, row = split_tile(t, per_angle)
        g = away(g, me, groups)
        word = e + s * SLOT_BIT + row * TILE_BIT
        waiting = open_tile[t]
        paired = waiting >= 0
        m = lists[g]
        at = list_base(g) + 2 * m
        lists[at] = waiting
        lists[at + 1] = word
        lists[g] = m + jnp.logical_and(paired, is_live).astype(jnp.int32)
        open_tile[t] = jnp.where(is_live, jnp.where(paired, -1, word), waiting)

    for c in range(parts):
        large[c].wait()

        @pl.when(edges[c] < live)
        def _(c=c):
            for e in range(edges[c], edges[c + 1]):
                work(e)

    for t in range(tile_rows):
        waiting = open_tile[t]
        g = away(split_tile(jnp.int32(t), per_angle)[0], me, groups)
        m = lists[g]
        at = list_base(g) + 2 * m
        lists[at] = waiting
        lists[at + 1] = slot_count * SLOT_BIT
        lists[g] = m + (waiting >= 0).astype(jnp.int32)
    for g in range(groups):
        at = list_base(g) + 2 * lists[g]
        for u in range(BACKWARD_PAIRS):
            lists[at + 2 * u] = per_angle * TILE_BIT
            lists[at + 2 * u + 1] = 0
    for s in range(slot_count):
        partial_out[s] = total[s].T.astype(partial_out.dtype)


def project(ray_of, received, total):
    total[...] = jnp.zeros_like(total)
    for r in range(received.shape[0]):
        total[ray_of[r]] += received[r].astype(jnp.float32)


def outgoing_kernel(ray_of, received, sinogram, ray_weight, outgoing, total, rounded):
    project(ray_of, received, total)
    rounded[...] = (ray_weight[...][:, None, :] * (sinogram[...] - total[...])).astype(rounded.dtype)
    for r in range(received.shape[0]):
        outgoing[r] = rounded[ray_of[r]]


def backward_sums(mask, groups, per_angle, lists, kept, returned, rows, total):
    slot_count = returned.shape[0]
    room = (lists.shape[0] - groups) // (2 * groups)
    rows[pl.ds(0, slot_count)] = returned[...]
    rows[slot_count] = jnp.zeros(rows.shape[1:], rows.dtype)
    total[...] = jnp.zeros_like(total)
    first = groups + mask * (2 * room)

    def multiply(i, _):
        for u in range(BACKWARD_PAIRS):
            at = first + 2 * (i * BACKWARD_PAIRS + u)
            one, two = lists[at], lists[at + 1]
            left = jnp.concatenate([rows[slot_bits(one)], rows[slot_bits(two)]], axis=1)
            right = jnp.concatenate([kept[entry_bits(one)], kept[entry_bits(two)]], axis=0)
            total[lax.shift_right_logical(one, 24)] += dot(left, right)
        return 0

    lax.fori_loop(0, ceil_div(lists[mask], BACKWARD_PAIRS), multiply, 0)
    return total[pl.ds(0, per_angle)]


def backward_kernel(mask, groups, lists, kept, returned, out, rows, total):
    out[...] = backward_sums(mask, groups, out.shape[0], lists, kept, returned, rows, total).astype(out.dtype)


def join_kernel(n_recv, share, *refs):
    recv, out = refs[:n_recv], refs[n_recv]
    value = share[...]
    for piece in recv:
        value = value + piece[...].astype(jnp.float32)
    out[...] = value.astype(out.dtype)


def own_kernel(groups, lists, ray_of, kept, returned, received, sinogram, ray_weight, volume_hbm, weight_hbm,
               out, weight_out, residual, rows, volume, weight, total, rays, sems):
    per_angle = out.shape[0]
    mine = pl.ds(lax.axis_index("angle").astype(jnp.int32) * per_angle, per_angle)
    copies = [
        pltpu.make_async_copy(volume_hbm.at[mine], volume, sems.at[0]),
        pltpu.make_async_copy(weight_hbm, weight, sems.at[1]),
    ]
    for copy in copies:
        copy.start()
    project(ray_of, received, rays)
    rays[...] = ray_weight[...][:, None, :] * (sinogram[...] - rays[...])
    away_copy = pltpu.make_async_copy(rays, residual, sems.at[2])
    away_copy.start()
    value = backward_sums(0, groups, per_angle, lists, kept, returned, rows, total)
    for copy in copies:
        copy.wait()
    scale = weight[mine][:, None, :]
    weight_out[...] = scale
    out[...] = volume[...] + scale * value
    away_copy.wait()


def update_kernel(n_recv, own, weight, *refs):
    recv, out = refs[:n_recv], refs[n_recv]
    value = recv[0][...].astype(jnp.float32)
    for piece in recv[1:]:
        value = value + piece[...].astype(jnp.float32)
    out[...] = own[...] + weight[...] * value


def body(volume, blocks, tile_of, slot_of, live_count, ray_of, sinogram, ray_weight, pixel_weight):
    n_region = lax.axis_size("region")
    n_angle = lax.axis_size("angle")
    slot_count = ray_of.shape[0]
    capacity = slot_count // n_region
    ray_rows = sinogram.shape[0]
    tile_rows, slices, pixels = volume.shape
    entries, rays, _ = blocks.shape
    per_angle = tile_rows // n_angle
    f32, bf16, i32 = jnp.float32, jnp.bfloat16, jnp.int32
    room = entries // 2 + per_angle + BACKWARD_PAIRS
    parts = min(FORWARD_PARTS, entries)
    params = pltpu.CompilerParams(vmem_limit_bytes=VMEM_LIMIT)
    in_hbm = functools.partial(pltpu.with_memory_space_constraint, memory_space=pltpu.HBM)
    in_vmem = functools.partial(pltpu.with_memory_space_constraint, memory_space=pltpu.VMEM)
    list_size = n_angle * (2 * room + 1)

    space = pl.pallas_call(
        lambda _: None,
        out_shape=pltpu.VMEM(blocks.shape, bf16),
        out_specs=pl.BlockSpec(memory_space=pl.ANY),
        compiler_params=params,
        name="space",
    )()
    partial_value, lists, rays_of, kept = pl.pallas_call(
        functools.partial(forward_kernel, per_angle, n_angle, room),
        out_shape=(
            MAYBE_HBM((slot_count, slices, rays), bf16),
            pltpu.SMEM((list_size,), i32),
            pltpu.SMEM((slot_count,), i32),
            pltpu.VMEM(blocks.shape, bf16),
        ),
        in_specs=[SMEM_SPEC] + [HBM_SPEC] * 5 + [VMEM_SPEC],
        out_specs=(VMEM_SPEC, SMEM_SPEC, SMEM_SPEC, pl.BlockSpec(memory_space=pl.ANY)),
        scratch_shapes=[
            pltpu.SMEM((entries,), i32),
            pltpu.SMEM((entries,), i32),
            pltpu.VMEM((tile_rows, slices, pixels), f32),
            pltpu.VMEM((tile_rows, slices, pixels), bf16),
            pltpu.VMEM((slot_count + 1, slices, rays), f32),
            pltpu.SMEM((tile_rows,), i32),
            pltpu.SemaphoreType.DMA((4,)),
            pltpu.SemaphoreType.DMA((parts,)),
        ],
        input_output_aliases={6: 3},
        compiler_params=params,
        name="forward",
    )(live_count, *[in_hbm(x) for x in (tile_of, slot_of, ray_of, volume, blocks)], in_vmem(space))

    received = lax.all_to_all(
        partial_value.reshape((n_region, capacity, slices, rays)), "region", split_axis=0, concat_axis=0, tiled=True
    ).reshape(slot_count, slices, rays)

    outgoing = pl.pallas_call(
        outgoing_kernel,
        out_shape=jax.ShapeDtypeStruct((slot_count, slices, rays), bf16),
        in_specs=[SMEM_SPEC, VMEM_SPEC, VMEM_SPEC, VMEM_SPEC],
        out_specs=VMEM_SPEC,
        scratch_shapes=[
            pltpu.VMEM((ray_rows, slices, rays), f32),
            pltpu.VMEM((ray_rows, slices, rays), bf16),
        ],
        compiler_params=params,
        name="outgoing",
    )(rays_of, received, sinogram, ray_weight)

    returned = lax.all_to_all(
        outgoing.reshape((n_region, capacity, slices, rays)), "region", split_axis=0, concat_axis=0, tiled=True
    ).reshape(slot_count, slices, rays)

    kept = in_vmem(kept)
    tile_shape = (per_angle, slices, pixels)
    work = [pltpu.VMEM((slot_count + 1, slices, rays), bf16), pltpu.VMEM((per_angle + 1, slices, pixels), f32)]

    def backward(mask, rows, out_type):
        return pl.pallas_call(
            functools.partial(backward_kernel, mask, n_angle),
            out_shape=jax.ShapeDtypeStruct(tile_shape, out_type),
            in_specs=[SMEM_SPEC] + [VMEM_SPEC] * 2,
            out_specs=VMEM_SPEC,
            scratch_shapes=work,
            compiler_params=params,
            name=f"backward_{mask}",
        )(lists, kept, rows)

    paired = n_angle & (n_angle - 1) == 0
    inbox = {m: [] for m in range(n_angle)}
    rows = returned
    def send(mask, rows):
        recv = inbox[mask]
        share = backward(mask, rows, f32 if recv else bf16)
        if recv:
            share = pl.pallas_call(
                functools.partial(join_kernel, len(recv)),
                out_shape=jax.ShapeDtypeStruct(tile_shape, bf16),
                in_specs=[VMEM_SPEC] * (1 + len(recv)),
                out_specs=VMEM_SPEC,
                compiler_params=params,
                name=f"join_{mask}",
            )(share, *recv)
            share, rows = lax.optimization_barrier((share, rows))
        hop = mask & -mask if paired else mask
        there = [(j, j ^ hop if paired else (j + hop) % n_angle) for j in range(n_angle)]
        inbox[mask ^ hop if paired else 0].append(lax.ppermute(share, "angle", there))
        return rows

    for mask in range(n_angle - 1, 1, -1):
        rows = send(mask, rows)
    own, weight, residual = pl.pallas_call(
        functools.partial(own_kernel, n_angle),
        out_shape=(
            jax.ShapeDtypeStruct(tile_shape, f32),
            jax.ShapeDtypeStruct((per_angle, 1, pixels), f32),
            jax.ShapeDtypeStruct((ray_rows, slices, rays), f32),
        ),
        in_specs=[SMEM_SPEC] * 2 + [VMEM_SPEC] * 5 + [HBM_SPEC] * 2,
        out_specs=(VMEM_SPEC, VMEM_SPEC, HBM_SPEC),
        scratch_shapes=[
            work[0],
            pltpu.VMEM(tile_shape, f32),
            pltpu.VMEM(pixel_weight.shape, f32),
            work[1],
            pltpu.VMEM((ray_rows, slices, rays), f32),
            pltpu.SemaphoreType.DMA((3,)),
        ],
        compiler_params=params,
        name="own",
    )(lists, rays_of, kept, rows, received, sinogram, ray_weight, in_hbm(volume), in_hbm(pixel_weight))
    rows, own = lax.optimization_barrier((rows, own))
    send(1, rows)
    recv = inbox[0]
    updated = pl.pallas_call(
        functools.partial(update_kernel, len(recv)),
        out_shape=jax.ShapeDtypeStruct((per_angle, slices, pixels), f32),
        in_specs=[VMEM_SPEC] * (len(recv) + 2),
        out_specs=VMEM_SPEC,
        compiler_params=params,
        name="update",
    )(own, weight, *recv)
    return (updated, residual)


def solution(mesh):
    placed = (
        P("region", None, None),
        P(("region", "angle"), None, None),
        P(("region", "angle")),
        P(("region", "angle")),
        P(("region", "angle")),
        P(("region", "angle")),
        P(("region", "angle"), None, None),
        P(("region", "angle"), None),
        P("region", None),
    )
    return jax.shard_map(
        body,
        mesh=mesh,
        in_specs=placed,
        out_specs=(P(("region", "angle"), None, None), P(("region", "angle"), None, None)),
        check_vma=False,
    )
```

```python
import functools

import jax
import jax.numpy as jnp
from jax import lax
from jax.experimental import pallas as pl
from jax.experimental.pallas import tpu as pltpu
from jax.sharding import PartitionSpec as P

FORWARD_PARTS = 3
BACKWARD_PAIRS = 12
SLOT_BIT = 1 << 16
TILE_BIT = 1 << 24
VMEM_LIMIT = 24 * 1024 * 1024
SMEM_SPEC = pl.BlockSpec(memory_space=pltpu.SMEM)
VMEM_SPEC = pl.BlockSpec(memory_space=pltpu.VMEM)
MAYBE_HBM = jax.ShapeDtypeStruct
HBM_SPEC = pl.BlockSpec(memory_space=pltpu.HBM)


def dot(x, y):
    return lax.dot_general(x, y, (((1,), (0,)), ((), ())), preferred_element_type=jnp.float32)


def ceil_div(a, b):
    return lax.div(a + (b - 1), jnp.int32(b))


def split_tile(tile, per_angle):
    if per_angle & (per_angle - 1) == 0:
        return lax.shift_right_logical(tile, per_angle.bit_length() - 1), jnp.bitwise_and(tile, per_angle - 1)
    return lax.div(tile, jnp.int32(per_angle)), lax.rem(tile, jnp.int32(per_angle))


def entry_bits(word):
    return jnp.bitwise_and(word, SLOT_BIT - 1)


def slot_bits(word):
    return jnp.bitwise_and(lax.shift_right_logical(word, 16), 255)


def away(group, me, groups):
    if groups & (groups - 1) == 0:
        return jnp.bitwise_xor(group, me)
    return lax.rem(group - me + groups, jnp.int32(groups))


def forward_kernel(per_angle, groups, room, live_count, tile_hbm, slot_hbm, ray_hbm, volume_hbm, blocks_hbm, held,
                   partial_out, lists, rays, kept, tile_of, slot_of, volume, volume_b, total, open_tile, sems, block_sems):
    entries = blocks_hbm.shape[0]
    slot_count, tile_rows = partial_out.shape[0], volume.shape[0]
    parts = block_sems.shape[0]
    edges = [entries * c // parts for c in range(parts + 1)]
    small = [
        pltpu.make_async_copy(slot_hbm, slot_of, sems.at[0]),
        pltpu.make_async_copy(tile_hbm, tile_of, sems.at[1]),
        pltpu.make_async_copy(volume_hbm, volume, sems.at[2]),
        pltpu.make_async_copy(ray_hbm, rays, sems.at[3]),
    ]
    large = []
    for c in range(parts):
        part = pl.ds(edges[c], edges[c + 1] - edges[c])
        large.append(pltpu.make_async_copy(blocks_hbm.at[part], kept.at[part], block_sems.at[c]))
    for copy in small + large:
        copy.start()
    me = lax.axis_index("angle").astype(jnp.int32)
    total[...] = jnp.zeros_like(total)
    for g in range(groups):
        lists[g] = 0
    for t in range(tile_rows):
        open_tile[t] = -1
    for copy in small:
        copy.wait()
    live = live_count[0]
    for t in range(tile_rows):
        volume_b[t] = volume[t].T.astype(jnp.bfloat16)

    def list_base(g):
        return groups + g * (2 * room)

    def work(e):
        is_live = e < live
        s, t = slot_of[e], tile_of[e]
        total[jnp.where(is_live, s, slot_count)] += dot(held[e], volume_b[t])
        g, row = split_tile(t, per_angle)
        g = away(g, me, groups)
        word = e + s * SLOT_BIT + row * TILE_BIT
        waiting = open_tile[t]
        paired = waiting >= 0
        m = lists[g]
        at = list_base(g) + 2 * m
        lists[at] = waiting
        lists[at + 1] = word
        lists[g] = m + jnp.logical_and(paired, is_live).astype(jnp.int32)
        open_tile[t] = jnp.where(is_live, jnp.where(paired, -1, word), waiting)

    for c in range(parts):
        large[c].wait()

        @pl.when(edges[c] < live)
        def _(c=c):
            for e in range(edges[c], edges[c + 1]):
                work(e)

    for t in range(tile_rows):
        waiting = open_tile[t]
        g = away(split_tile(jnp.int32(t), per_angle)[0], me, groups)
        m = lists[g]
        at = list_base(g) + 2 * m
        lists[at] = waiting
        lists[at + 1] = slot_count * SLOT_BIT
        lists[g] = m + (waiting >= 0).astype(jnp.int32)
    for g in range(groups):
        at = list_base(g) + 2 * lists[g]
        for u in range(BACKWARD_PAIRS):
            lists[at + 2 * u] = per_angle * TILE_BIT
            lists[at + 2 * u + 1] = 0
    for s in range(slot_count):
        partial_out[s] = total[s].T.astype(partial_out.dtype)


def project(ray_of, received, total):
    total[...] = jnp.zeros_like(total)
    for r in range(received.shape[0]):
        total[ray_of[r]] += received[r].astype(jnp.float32)


def outgoing_kernel(ray_of, received, sinogram, ray_weight, outgoing, total, rounded):
    project(ray_of, received, total)
    rounded[...] = (ray_weight[...][:, None, :] * (sinogram[...] - total[...])).astype(rounded.dtype)
    for r in range(received.shape[0]):
        outgoing[r] = rounded[ray_of[r]]


def backward_sums(mask, groups, per_angle, lists, kept, returned, rows, total):
    slot_count = returned.shape[0]
    room = (lists.shape[0] - groups) // (2 * groups)
    rows[pl.ds(0, slot_count)] = returned[...]
    rows[slot_count] = jnp.zeros(rows.shape[1:], rows.dtype)
    total[...] = jnp.zeros_like(total)
    first = groups + mask * (2 * room)

    def multiply(i, _):
        for u in range(BACKWARD_PAIRS):
            at = first + 2 * (i * BACKWARD_PAIRS + u)
            one, two = lists[at], lists[at + 1]
            left = jnp.concatenate([rows[slot_bits(one)], rows[slot_bits(two)]], axis=1)
            right = jnp.concatenate([kept[entry_bits(one)], kept[entry_bits(two)]], axis=0)
            total[lax.shift_right_logical(one, 24)] += dot(left, right)
        return 0

    lax.fori_loop(0, ceil_div(lists[mask], BACKWARD_PAIRS), multiply, 0)
    return total[pl.ds(0, per_angle)]


def backward_kernel(mask, groups, lists, kept, returned, out, rows, total):
    out[...] = backward_sums(mask, groups, out.shape[0], lists, kept, returned, rows, total).astype(out.dtype)


def join_kernel(n_recv, share, *refs):
    recv, out = refs[:n_recv], refs[n_recv]
    value = share[...]
    for piece in recv:
        value = value + piece[...].astype(jnp.float32)
    out[...] = value.astype(out.dtype)


def own_kernel(groups, lists, ray_of, kept, returned, received, sinogram, ray_weight, volume_hbm, weight_hbm,
               out, weight_out, residual, rows, volume, weight, total, rays, sems):
    per_angle = out.shape[0]
    mine = pl.ds(lax.axis_index("angle").astype(jnp.int32) * per_angle, per_angle)
    copies = [
        pltpu.make_async_copy(volume_hbm.at[mine], volume, sems.at[0]),
        pltpu.make_async_copy(weight_hbm, weight, sems.at[1]),
    ]
    for copy in copies:
        copy.start()
    project(ray_of, received, rays)
    rays[...] = ray_weight[...][:, None, :] * (sinogram[...] - rays[...])
    away_copy = pltpu.make_async_copy(rays, residual, sems.at[2])
    away_copy.start()
    value = backward_sums(0, groups, per_angle, lists, kept, returned, rows, total)
    for copy in copies:
        copy.wait()
    scale = weight[mine][:, None, :]
    weight_out[...] = scale
    out[...] = volume[...] + scale * value
    away_copy.wait()


def update_kernel(n_recv, own, weight, *refs):
    recv, out = refs[:n_recv], refs[n_recv]
    value = recv[0][...].astype(jnp.float32)
    for piece in recv[1:]:
        value = value + piece[...].astype(jnp.float32)
    out[...] = own[...] + weight[...] * value


def body(volume, blocks, tile_of, slot_of, live_count, ray_of, sinogram, ray_weight, pixel_weight):
    n_region = lax.axis_size("region")
    n_angle = lax.axis_size("angle")
    slot_count = ray_of.shape[0]
    capacity = slot_count // n_region
    ray_rows = sinogram.shape[0]
    tile_rows, slices, pixels = volume.shape
    entries, rays, _ = blocks.shape
    per_angle = tile_rows // n_angle
    f32, bf16, i32 = jnp.float32, jnp.bfloat16, jnp.int32
    room = entries // 2 + per_angle + BACKWARD_PAIRS
    parts = min(FORWARD_PARTS, entries)
    params = pltpu.CompilerParams(vmem_limit_bytes=VMEM_LIMIT)
    in_hbm = functools.partial(pltpu.with_memory_space_constraint, memory_space=pltpu.HBM)
    in_vmem = functools.partial(pltpu.with_memory_space_constraint, memory_space=pltpu.VMEM)
    list_size = n_angle * (2 * room + 1)

    space = pl.pallas_call(
        lambda _: None,
        out_shape=pltpu.VMEM(blocks.shape, bf16),
        out_specs=pl.BlockSpec(memory_space=pl.ANY),
        compiler_params=params,
        name="space",
    )()
    partial_value, lists, rays_of, kept = pl.pallas_call(
        functools.partial(forward_kernel, per_angle, n_angle, room),
        out_shape=(
            MAYBE_HBM((slot_count, slices, rays), bf16),
            pltpu.SMEM((list_size,), i32),
            pltpu.SMEM((slot_count,), i32),
            pltpu.VMEM(blocks.shape, bf16),
        ),
        in_specs=[SMEM_SPEC] + [HBM_SPEC] * 5 + [VMEM_SPEC],
        out_specs=(VMEM_SPEC, SMEM_SPEC, SMEM_SPEC, pl.BlockSpec(memory_space=pl.ANY)),
        scratch_shapes=[
            pltpu.SMEM((entries,), i32),
            pltpu.SMEM((entries,), i32),
            pltpu.VMEM((tile_rows, slices, pixels), f32),
            pltpu.VMEM((tile_rows, slices, pixels), bf16),
            pltpu.VMEM((slot_count + 1, slices, rays), f32),
            pltpu.SMEM((tile_rows,), i32),
            pltpu.SemaphoreType.DMA((4,)),
            pltpu.SemaphoreType.DMA((parts,)),
        ],
        input_output_aliases={6: 3},
        compiler_params=params,
        name="forward",
    )(live_count, *[in_hbm(x) for x in (tile_of, slot_of, ray_of, volume, blocks)], in_vmem(space))

    received = lax.all_to_all(
        partial_value.reshape((n_region, capacity, slices, rays)), "region", split_axis=0, concat_axis=0, tiled=True
    ).reshape(slot_count, slices, rays)

    outgoing = pl.pallas_call(
        outgoing_kernel,
        out_shape=jax.ShapeDtypeStruct((slot_count, slices, rays), bf16),
        in_specs=[SMEM_SPEC, VMEM_SPEC, VMEM_SPEC, VMEM_SPEC],
        out_specs=VMEM_SPEC,
        scratch_shapes=[
            pltpu.VMEM((ray_rows, slices, rays), f32),
            pltpu.VMEM((ray_rows, slices, rays), bf16),
        ],
        compiler_params=params,
        name="outgoing",
    )(rays_of, received, sinogram, ray_weight)

    returned = lax.all_to_all(
        outgoing.reshape((n_region, capacity, slices, rays)), "region", split_axis=0, concat_axis=0, tiled=True
    ).reshape(slot_count, slices, rays)

    kept = in_vmem(kept)
    tile_shape = (per_angle, slices, pixels)
    work = [pltpu.VMEM((slot_count + 1, slices, rays), bf16), pltpu.VMEM((per_angle + 1, slices, pixels), f32)]

    def backward(mask, rows, out_type):
        return pl.pallas_call(
            functools.partial(backward_kernel, mask, n_angle),
            out_shape=jax.ShapeDtypeStruct(tile_shape, out_type),
            in_specs=[SMEM_SPEC] + [VMEM_SPEC] * 2,
            out_specs=VMEM_SPEC,
            scratch_shapes=work,
            compiler_params=params,
            name=f"backward_{mask}",
        )(lists, kept, rows)

    paired = n_angle & (n_angle - 1) == 0
    inbox = {m: [] for m in range(n_angle)}
    rows = returned
    def send(mask, rows):
        recv = inbox[mask]
        share = backward(mask, rows, f32 if recv else bf16)
        if recv:
            share = pl.pallas_call(
                functools.partial(join_kernel, len(recv)),
                out_shape=jax.ShapeDtypeStruct(tile_shape, bf16),
                in_specs=[VMEM_SPEC] * (1 + len(recv)),
                out_specs=VMEM_SPEC,
                compiler_params=params,
                name=f"join_{mask}",
            )(share, *recv)
            share, rows = lax.optimization_barrier((share, rows))
        hop = mask & -mask if paired else mask
        there = [(j, j ^ hop if paired else (j + hop) % n_angle) for j in range(n_angle)]
        inbox[mask ^ hop if paired else 0].append(lax.ppermute(share, "angle", there))
        return rows

    for mask in range(n_angle - 1, 1, -1):
        rows = send(mask, rows)
    own, weight, residual = pl.pallas_call(
        functools.partial(own_kernel, n_angle),
        out_shape=(
            jax.ShapeDtypeStruct(tile_shape, f32),
            jax.ShapeDtypeStruct((per_angle, 1, pixels), f32),
            jax.ShapeDtypeStruct((ray_rows, slices, rays), f32),
        ),
        in_specs=[SMEM_SPEC] * 2 + [VMEM_SPEC] * 5 + [HBM_SPEC] * 2,
        out_specs=(VMEM_SPEC, VMEM_SPEC, HBM_SPEC),
        scratch_shapes=[
            work[0],
            pltpu.VMEM(tile_shape, f32),
            pltpu.VMEM(pixel_weight.shape, f32),
            work[1],
            pltpu.VMEM((ray_rows, slices, rays), f32),
            pltpu.SemaphoreType.DMA((3,)),
        ],
        compiler_params=params,
        name="own",
    )(lists, rays_of, kept, rows, received, sinogram, ray_weight, in_hbm(volume), in_hbm(pixel_weight))
    rows, own = lax.optimization_barrier((rows, own))
    send(1, rows)
    recv = inbox[0]
    updated = pl.pallas_call(
        functools.partial(update_kernel, len(recv)),
        out_shape=jax.ShapeDtypeStruct((per_angle, slices, pixels), f32),
        in_specs=[VMEM_SPEC] * (len(recv) + 2),
        out_specs=VMEM_SPEC,
        compiler_params=params,
        name="update",
    )(own, weight, *recv)
    return (updated, residual)


def solution(mesh):
    placed = (
        P("region", None, None),
        P(("region", "angle"), None, None),
        P(("region", "angle")),
        P(("region", "angle")),
        P(("region", "angle")),
        P(("region", "angle")),
        P(("region", "angle"), None, None),
        P(("region", "angle"), None),
        P("region", None),
    )
    return jax.shard_map(
        body,
        mesh=mesh,
        in_specs=placed,
        out_specs=(P(("region", "angle"), None, None), P(("region", "angle"), None, None)),
        check_vma=False,
    )
```
